768 devices in a mesh: dp: 32 (over x, y), fsdp: 4 (over z_hi), sub: 6 (over z_lo, core).
Axes of the slice: x: 4, y: 8, z: 12 (z_hi: 4, z_lo: 3; z = z_hi * 3 + z_lo), core: 2. Of those that a mesh axis runs over, the one named last changes fastest.
Arguments:
- grads: bfloat16 [192, 3, 1024, 1024], P(('dp', 'sub'), None, 'fsdp'), may hold values from -0.109375 to 0.109375
- owner_block: int32 [32], replicated, may hold values from -1 to 2, as said below
- left_stat: float32 [32, 1024, 1024], P('dp', 'fsdp'), as said below
- right_stat: float32 [32, 1024, 1024], P('dp', 'fsdp'), as said below
- left_root: bfloat16 [32, 1024, 1024], P('dp', 'fsdp'), as said below
- right_root: bfloat16 [32, 1024, 1024], P('dp'), as said below
Outputs:
- update: bfloat16 [3, 1024, 1024], P(None, 'fsdp')
- new_left: float32 [32, 1024, 1024], P('dp', 'fsdp')
- new_right: float32 [32, 1024, 1024], P('dp', 'fsdp')
The draws below stay inside these ranges and needn't reach their ends.
Inputs may be any that keep to these rules, and one draw needn't show every extreme that they name: `owner_block`: each of the block numbers 0 to 2 stands at exactly one dp index; all other entries are -1. `left_stat`: symmetric. `right_stat`: symmetric. `left_root`: symmetric. `right_root`: symmetric.
All inputs are finite; a program needn't handle non-finite values.
Results may differ from the reference program's by a relative error of at most 0.024.
Values may be sent and summed in bfloat16 or wider, within the bound.
No kernel may reach another device: no remote copies, remote signals or barrier semaphores. Data moves between devices by JAX's collectives and lax.ppermute only.
A program may use at most 64 MiB of HBM per device.

```python
import jax
import jax.numpy as jnp
from jax import lax

BLOCK = 1024
NB = 3
REPLICAS = 192
N_DP = 32
N_SUB = 6


def shape_up(noise, diag):
    sym = (noise + jnp.swapaxes(noise, 1, 2)) * 0.5
    eye = jnp.eye(BLOCK, dtype=jnp.float32)
    return sym + eye[None, :, :] * diag[:, None, :]


def draw_owner_block(key, part):
    key = jax.random.fold_in(key, 1)
    order = jax.random.permutation(key, N_DP)
    return jnp.where(order < NB, order, -1).astype(jnp.int32)


def draw_left_stat(key, part):
    key = jax.random.fold_in(key, 2)
    first, second = jax.random.split(key)
    noise = jax.random.normal(first, (N_DP, BLOCK, BLOCK), jnp.float32) * 0.1
    diag = jnp.exp(jax.random.uniform(second, (N_DP, BLOCK), jnp.float32, 0.0, 2.3))
    return shape_up(noise, diag)


def draw_right_stat(key, part):
    key = jax.random.fold_in(key, 3)
    first, second = jax.random.split(key)
    noise = jax.random.normal(first, (N_DP, BLOCK, BLOCK), jnp.float32) * 0.1
    diag = jnp.exp(jax.random.uniform(second, (N_DP, BLOCK), jnp.float32, 0.0, 2.3))
    return shape_up(noise, diag)


def draw_left_root(key, part):
    key = jax.random.fold_in(key, 4)
    first, second = jax.random.split(key)
    noise = jax.random.normal(first, (N_DP, BLOCK, BLOCK), jnp.float32) * 0.008
    diag = jnp.exp(jax.random.uniform(second, (N_DP, BLOCK), jnp.float32, -0.69, 0.69))
    return shape_up(noise, diag).astype(jnp.bfloat16)


def draw_right_root(key, part):
    key = jax.random.fold_in(key, 5)
    first, second = jax.random.split(key)
    noise = jax.random.normal(first, (N_DP, BLOCK, BLOCK), jnp.float32) * 0.008
    diag = jnp.exp(jax.random.uniform(second, (N_DP, BLOCK), jnp.float32, -0.69, 0.69))
    return shape_up(noise, diag).astype(jnp.bfloat16)


def block_levels(rng, shape, cuts, smallest, largest):
    gain, own = 1.0, jax.random.fold_in(rng, 6)
    for dim, blocks in cuts:
        steps = jnp.exp(jax.random.uniform(jax.random.fold_in(own, dim), (blocks,), jnp.float32, smallest / len(cuts), largest / len(cuts)))
        gain = gain * jnp.repeat(steps, shape[dim] // blocks).reshape([-1 if axis == dim else 1 for axis in range(len(shape))])
    return gain


def scatter_about(key, shape, deviation, bound, cuts=(), kind=jnp.bfloat16):
    level = block_levels(key, shape, cuts, -0.22, 0.18) if cuts else 1.0
    drawn = jax.random.normal(key, shape, jnp.float32) * deviation * level
    return jnp.minimum(jnp.maximum(drawn, -bound), bound).astype(kind)


def setup_inputs(seed: int = 0) -> dict:
    seeds = jax.random.split(jax.random.key(seed), 7)
    return {
        "grads": scatter_about(seeds[0], (REPLICAS, NB, BLOCK, BLOCK), (0.25 * (N_DP * N_SUB) ** -0.5), 0.109375, ((0, 192), (2, 4))),
        "owner_block": draw_owner_block(jax.random.fold_in(seeds[6], 71), 0),
        "left_stat": draw_left_stat(jax.random.fold_in(seeds[6], 71), 0),
        "right_stat": draw_right_stat(jax.random.fold_in(seeds[6], 71), 0),
        "left_root": draw_left_root(jax.random.fold_in(seeds[6], 71), 0),
        "right_root": draw_right_root(jax.random.fold_in(seeds[6], 71), 0),
    }


BETA = 0.95


def reference(grads, owner_block, left_stat, right_stat, left_root, right_root):
    new_left = left_stat
    new_right = right_stat
    results = []
    for block in range(NB):
        def accumulate(index, total):
            replica = lax.dynamic_index_in_dim(grads, index, 0, False)
            return total + replica[block].astype(jnp.float32)

        summed = lax.fori_loop(0, grads.shape[0], accumulate, jnp.zeros((BLOCK, BLOCK), jnp.float32))
        grad_sum = summed.astype(jnp.bfloat16)
        owner = jnp.argmax(owner_block == block).astype(jnp.int32)
        outer_left = jnp.dot(grad_sum, grad_sum.T, preferred_element_type=jnp.float32)
        outer_right = jnp.dot(grad_sum.T, grad_sum, preferred_element_type=jnp.float32)
        new_left = new_left.at[owner].set(BETA * left_stat[owner] + (1.0 - BETA) * outer_left)
        new_right = new_right.at[owner].set(BETA * right_stat[owner] + (1.0 - BETA) * outer_right)
        left_side = jnp.dot(left_root[owner], grad_sum, preferred_element_type=jnp.float32).astype(jnp.bfloat16)
        results.append(jnp.dot(left_side, right_root[owner], preferred_element_type=jnp.float32).astype(jnp.bfloat16))
    return jnp.stack(results), new_left, new_right
```

```python
import jax
import jax.numpy as jnp
from jax import lax
from jax.sharding import Mesh, PartitionSpec as P

BETA = 0.95
NX, NY = 4, 8
NZH, NZL, NC = 4, 3, 2
AXES = ("x", "y", "zh", "zl", "c")


def swap_cores(value):
    return lax.ppermute(value, "c", [(0, 1), (1, 0)])


def per_device(grads, owner_block, left_stat, right_stat, left_root, right_root):
    f32, bf16 = jnp.float32, jnp.bfloat16
    g = grads[0]
    blocks, rows, width = g.shape
    half = width // 2
    peers = NX * NY
    band = rows // peers
    core = lax.axis_index("c")
    first = core == 0
    low, high = g[:, :, :half], g[:, :, half:]

    got = swap_cores(jnp.where(first, high, low))
    mine_half = jnp.where(first, low, high)
    pair = (mine_half.astype(f32) + got.astype(f32)).astype(bf16)
    pieces = pair.reshape(blocks, peers, band, half).transpose(1, 0, 2, 3)
    arrived = lax.all_to_all(pieces, ("x", "y"), 0, 0, tiled=True)
    reduced = jnp.sum(arrived.astype(f32), axis=0).astype(bf16)

    spread = jnp.broadcast_to(reduced[None], (NZH * NZL,) + reduced.shape)
    column = lax.all_to_all(spread, ("zh", "zl"), 0, 0, tiled=True)
    column = jnp.sum(
        column.reshape((NZH, NZL) + reduced.shape).astype(f32), axis=1
    ).astype(bf16)

    want = owner_block[:, None, None, None]
    outgoing = jnp.where(
        want == 1, column[None, :, 1], jnp.where(want == 2, column[None, :, 2], column[None, :, 0])
    )
    mine = lax.all_to_all(outgoing, ("x", "y"), 0, 0, tiled=True)
    mine = mine.transpose(1, 0, 2, 3).reshape(NZH * rows, half)
    other = swap_cores(mine)
    whole = jnp.concatenate(
        [jnp.where(first, mine, other), jnp.where(first, other, mine)], axis=1
    )

    shard = lax.axis_index("zh")
    dp = lax.axis_index(("x", "y"))
    owner = lax.dynamic_index_in_dim(owner_block, dp, 0, False)
    owns = owner >= 0
    grad_rows = lax.dynamic_slice_in_dim(whole, shard * rows, rows, 0)
    columns = lax.dynamic_slice_in_dim(whole, shard * rows, rows, 1)
    left_side = jnp.dot(left_root[0], whole, preferred_element_type=f32).astype(bf16)
    root_half = lax.dynamic_slice_in_dim(right_root[0], core * half, half, 1)
    result = jnp.dot(left_side, root_half, preferred_element_type=f32).astype(bf16)

    scattered = lax.all_to_all(
        result.reshape(peers, band, half), ("x", "y"), 0, 0, tiled=True
    )
    placed = jnp.stack(
        [
            lax.dynamic_index_in_dim(
                scattered, jnp.argmax(owner_block == block), 0, False
            )
            for block in range(blocks)
        ]
    )
    spread = jnp.broadcast_to(placed[None], (peers,) + placed.shape)
    update_half = lax.all_to_all(spread, ("x", "y"), 0, 0, tiled=True)
    update_half = update_half.transpose(1, 0, 2, 3).reshape(blocks, rows, half)
    update_other = swap_cores(update_half)
    update = jnp.concatenate(
        [jnp.where(first, update_half, update_other), jnp.where(first, update_other, update_half)],
        axis=2,
    )

    left_old, right_old = left_stat[0], right_stat[0]

    def owned():
        outer_left = lax.dot_general(
            grad_rows, whole, (((1,), (1,)), ((), ())), preferred_element_type=f32
        )
        outer_right = lax.dot_general(
            columns, whole, (((0,), (0,)), ((), ())), preferred_element_type=f32
        )
        return (
            BETA * left_old + (1.0 - BETA) * outer_left,
            BETA * right_old + (1.0 - BETA) * outer_right,
        )

    new_left, new_right = lax.cond(owns, owned, lambda: (left_old, right_old))
    return update, new_left[None], new_right[None]


def solution(mesh):
    fine = Mesh(mesh.devices.reshape(NX, NY, NZH, NZL, NC), AXES)
    dp = ("x", "y")
    in_specs = (
        P(("x", "y", "zl", "c"), None, "zh", None),
        P(),
        P(dp, "zh", None),
        P(dp, "zh", None),
        P(dp, "zh", None),
        P(dp, None, None),
    )
    out_specs = (P(None, "zh", None), P(dp, "zh", None), P(dp, "zh", None))
    return jax.shard_map(
        per_device, mesh=fine, in_specs=in_specs, out_specs=out_specs, check_vma=False
    )
```

```python
import jax
import jax.numpy as jnp
from jax import lax
from jax.experimental import pallas as pl
from jax.experimental.pallas import tpu as pltpu
from jax.sharding import Mesh, PartitionSpec as P

BETA = 0.95
NX, NY = 4, 8
NZH, NZL, NC = 4, 3, 2
AXES = ("x", "y", "zh", "zl", "c")
DP = ("x", "y")


def swap_cores(value):
    return lax.ppermute(value, "c", [(0, 1), (1, 0)])


def stats_kernel(where, own, other, left_old, right_old, left_new, right_new, turned):
    shard, core, owns = where[0], where[1], where[2]
    rows = left_old.shape[0]
    half = own.shape[1]
    per_half = half // rows

    @pl.when(owns == 0)
    def _():
        left_new[...] = left_old[...]
        right_new[...] = right_old[...]

    @pl.when(owns != 0)
    def _():
        band = pl.ds(pl.multiple_of(shard * rows, rows), rows)
        outer = lax.dot_general(
            own[band, :], own[...], (((1,), (1,)), ((), ())), preferred_element_type=jnp.float32
        ) + lax.dot_general(
            other[band, :], other[...], (((1,), (1,)), ((), ())), preferred_element_type=jnp.float32
        )
        left_new[...] = BETA * left_old[...] + (1.0 - BETA) * outer
        columns = pl.ds(pl.multiple_of((shard % per_half) * rows, rows), rows)

        @pl.when(shard // per_half == core)
        def _():
            turned[...] = own[:, columns].T

        @pl.when(shard // per_half != core)
        def _():
            turned[...] = other[:, columns].T

        for source, place in ((own, core), (other, 1 - core)):
            span = pl.ds(pl.multiple_of(place * half, half), half)
            product = jnp.dot(turned[...], source[...], preferred_element_type=jnp.float32)
            right_new[:, span] = BETA * right_old[:, span] + (1.0 - BETA) * product


def update_stats(where, own, other, left_old, right_old):
    rows, width = left_old.shape
    vmem = pl.BlockSpec(memory_space=pltpu.VMEM)
    return pl.pallas_call(
        stats_kernel,
        out_shape=[jax.ShapeDtypeStruct((rows, width), jnp.float32)] * 2,
        in_specs=[pl.BlockSpec(memory_space=pltpu.SMEM)] + [vmem] * 4,
        out_specs=[vmem, vmem],
        scratch_shapes=[pltpu.VMEM((rows, width), jnp.bfloat16)],
        compiler_params=pltpu.CompilerParams(vmem_limit_bytes=24 * 1024 * 1024),
        cost_estimate=pl.CostEstimate(
            flops=4 * rows * width * width, bytes_accessed=24 * rows * width, transcendentals=0
        ),
    )(where, own, other, left_old, right_old)


def join_kernel(core, own, other, joined, sems):
    half = own.shape[2]
    copies = [
        pltpu.make_async_copy(
            source, joined.at[:, :, pl.ds(pl.multiple_of(place * half, half), half)], sems.at[n]
        )
        for n, (source, place) in enumerate(((own, core[0]), (other, 1 - core[0])))
    ]
    for copy in copies:
        copy.start()
    for copy in copies:
        copy.wait()


def join_halves(core, own, other):
    blocks, rows, half = own.shape
    anywhere = pl.BlockSpec(memory_space=pl.ANY)
    return pl.pallas_call(
        join_kernel,
        out_shape=jax.ShapeDtypeStruct((blocks, rows, 2 * half), own.dtype),
        in_specs=[pl.BlockSpec(memory_space=pltpu.SMEM), anywhere, anywhere],
        out_specs=anywhere,
        scratch_shapes=[pltpu.SemaphoreType.DMA((2,))],
    )(core, own, other)


def per_device(grads, owner_block, left_stat, right_stat, left_root, right_root):
    f32, bf16 = jnp.float32, jnp.bfloat16
    g = grads[0]
    blocks, rows, width = g.shape
    half = width // 2
    peers = NX * NY
    band = rows // peers
    core = lax.axis_index("c")
    shard = lax.axis_index("zh")
    dp = lax.axis_index(DP)
    owns = lax.dynamic_index_in_dim(owner_block, dp, 0, False) >= 0

    got = swap_cores(lax.dynamic_slice_in_dim(g, (1 - core) * half, half, 2))
    kept = lax.dynamic_slice_in_dim(g, core * half, half, 2)
    pair = (kept.astype(f32) + got.astype(f32)).astype(bf16)

    pieces = pair.reshape(blocks, peers, band, half).transpose(1, 0, 2, 3)
    arrived = lax.all_to_all(pieces.reshape(peers, blocks * band, half), DP, 0, 0, tiled=True)
    reduced = jnp.sum(arrived.astype(f32), axis=0).astype(bf16)

    spread = jnp.broadcast_to(reduced[None], (NZH * NZL,) + reduced.shape)
    column = lax.all_to_all(spread, ("zh", "zl"), 0, 0, tiled=True)
    column = jnp.sum(column.reshape((NZH, NZL) + reduced.shape).astype(f32), axis=1).astype(bf16)
    column = column.reshape(NZH, blocks, band, half)

    want = owner_block[:, None, None, None]
    outgoing = jnp.where(
        want == 1, column[None, :, 1], jnp.where(want == 2, column[None, :, 2], column[None, :, 0])
    )
    mine = lax.all_to_all(outgoing.reshape(peers, NZH * band, half), DP, 0, 0, tiled=True)
    mine = mine.reshape(peers, NZH, band, half).transpose(1, 0, 2, 3).reshape(NZH * rows, half)
    other = swap_cores(mine)

    side = jnp.dot(left_root[0], mine, preferred_element_type=f32).astype(bf16)
    side_other = swap_cores(side)
    root = lax.dynamic_slice_in_dim(right_root[0], core * half, half, 1)
    root_mine = lax.dynamic_slice_in_dim(root, core * half, half, 0)
    root_other = lax.dynamic_slice_in_dim(root, (1 - core) * half, half, 0)
    result = (
        jnp.dot(side, root_mine, preferred_element_type=f32)
        + jnp.dot(side_other, root_other, preferred_element_type=f32)
    ).astype(bf16)

    scattered = lax.all_to_all(result.reshape(peers, band, half), DP, 0, 0, tiled=True)
    where = jnp.stack([shard, core, owns.astype(jnp.int32)]).astype(jnp.int32)
    new_left, new_right = update_stats(where, mine, other, left_stat[0], right_stat[0])
    scattered, new_left, new_right = lax.optimization_barrier((scattered, new_left, new_right))
    placed = jnp.concatenate(
        [
            lax.dynamic_index_in_dim(scattered, jnp.argmax(owner_block == block), 0, False)
            for block in range(blocks)
        ]
    )
    spread = jnp.broadcast_to(placed[None], (peers,) + placed.shape)
    update_half = lax.all_to_all(spread, DP, 0, 0, tiled=True)
    update_half = update_half.reshape(peers, blocks, band, half)
    update_half = update_half.transpose(1, 0, 2, 3).reshape(blocks, rows, half)
    update = join_halves(core[None].astype(jnp.int32), update_half, swap_cores(update_half))

    return update, new_left[None], new_right[None]


def solution(mesh):
    fine = Mesh(mesh.devices.reshape(NX, NY, NZH, NZL, NC), AXES)
    in_specs = (
        P(("x", "y", "zl", "c"), None, "zh", None),
        P(),
        P(DP, "zh", None),
        P(DP, "zh", None),
        P(DP, "zh", None),
        P(DP, None, None),
    )
    out_specs = (P(None, "zh", None), P(DP, "zh", None), P(DP, "zh", None))
    return jax.shard_map(
        per_device, mesh=fine, in_specs=in_specs, out_specs=out_specs, check_vma=False
    )
```

```python
import jax
import jax.numpy as jnp
from jax import lax
from jax.experimental import pallas as pl
from jax.experimental.pallas import tpu as pltpu
from jax.sharding import Mesh, PartitionSpec as P

BETA = 0.95
NX, NY = 4, 8
NZH, NZL, NC = 4, 3, 2
AXES = ("x", "y", "zh", "zl", "c")
DP = ("x", "y")


def swap_cores(value):
    return lax.ppermute(value, "c", [(0, 1), (1, 0)])


def beside(operand, transfer, work, inputs):
    operand, inputs = lax.optimization_barrier((operand, inputs))
    return lax.optimization_barrier((transfer(operand), work(*inputs)))


def stats_kernel(where, own, other, left_old, right_old, left_new, right_new, turned):
    shard, core, owns = where[0], where[1], where[2]
    rows = left_old.shape[0]
    half = own.shape[1]
    per_half = half // rows

    @pl.when(owns == 0)
    def _():
        left_new[...] = left_old[...]
        right_new[...] = right_old[...]

    @pl.when(owns != 0)
    def _():
        band = pl.ds(pl.multiple_of(shard * rows, rows), rows)
        outer = lax.dot_general(
            own[band, :], own[...], (((1,), (1,)), ((), ())), preferred_element_type=jnp.float32
        ) + lax.dot_general(
            other[band, :], other[...], (((1,), (1,)), ((), ())), preferred_element_type=jnp.float32
        )
        left_new[...] = BETA * left_old[...] + (1.0 - BETA) * outer
        columns = pl.ds(pl.multiple_of((shard % per_half) * rows, rows), rows)

        @pl.when(shard // per_half == core)
        def _():
            turned[...] = own[:, columns].T

        @pl.when(shard // per_half != core)
        def _():
            turned[...] = other[:, columns].T

        for source, place in ((own, core), (other, 1 - core)):
            span = pl.ds(pl.multiple_of(place * half, half), half)
            product = jnp.dot(turned[...], source[...], preferred_element_type=jnp.float32)
            right_new[:, span] = BETA * right_old[:, span] + (1.0 - BETA) * product


def update_stats(where, own, other, left_old, right_old):
    rows, width = left_old.shape
    vmem = pl.BlockSpec(memory_space=pltpu.VMEM)
    return pl.pallas_call(
        stats_kernel,
        out_shape=[jax.ShapeDtypeStruct((rows, width), jnp.float32)] * 2,
        in_specs=[pl.BlockSpec(memory_space=pltpu.SMEM)] + [vmem] * 4,
        out_specs=[vmem, vmem],
        scratch_shapes=[pltpu.VMEM((rows, width), jnp.bfloat16)],
        compiler_params=pltpu.CompilerParams(vmem_limit_bytes=24 * 1024 * 1024),
        cost_estimate=pl.CostEstimate(
            flops=4 * rows * width * width, bytes_accessed=24 * rows * width, transcendentals=0
        ),
    )(where, own, other, left_old, right_old)


def join_kernel(core, own, other, joined):
    half = own.shape[2]
    for source, place in ((own, core[0]), (other, 1 - core[0])):
        joined[:, :, pl.ds(pl.multiple_of(place * half, half), half)] = source[...]


def join_halves(core, own, other):
    blocks, rows, half = own.shape
    vmem = pl.BlockSpec(memory_space=pltpu.VMEM)
    return pl.pallas_call(
        join_kernel,
        out_shape=jax.ShapeDtypeStruct((blocks, rows, 2 * half), own.dtype),
        in_specs=[pl.BlockSpec(memory_space=pltpu.SMEM), vmem, vmem],
        out_specs=vmem,
        compiler_params=pltpu.CompilerParams(vmem_limit_bytes=16 * 1024 * 1024),
    )(core, own, other)


def cut_root(root, core):
    half = root.shape[1] // 2
    root = lax.dynamic_slice_in_dim(root, core * half, half, 1)
    return (
        lax.dynamic_slice_in_dim(root, core * half, half, 0),
        lax.dynamic_slice_in_dim(root, (1 - core) * half, half, 0),
    )


def find(owners, shard, core, dp):
    owns = (lax.dynamic_index_in_dim(owners, dp, 0, False) >= 0).astype(jnp.int32)
    where = jnp.stack([shard, core, owns]).astype(jnp.int32)
    hits = owners[None, :] == jnp.arange(NZL, dtype=jnp.int32)[:, None]
    return where, jnp.argmax(hits, axis=1).astype(jnp.int32)


def per_device(grads, owner_block, left_stat, right_stat, left_root, right_root):
    f32, bf16 = jnp.float32, jnp.bfloat16
    g = grads[0]
    blocks, rows, width = g.shape
    half = width // 2
    peers = NX * NY
    band = rows // peers
    core = lax.axis_index("c")
    shard = lax.axis_index("zh")
    dp = lax.axis_index(DP)
    first = core == 0

    low, high = g[:, :, :half], g[:, :, half:]
    got = swap_cores(jnp.where(first, high, low))
    pair = (jnp.where(first, low, high).astype(f32) + got.astype(f32)).astype(bf16)

    arrived, (root_mine, root_other) = beside(
        pair.reshape(blocks * peers, band, half),
        lambda value: lax.all_to_all(value, ("zl",) + DP, 0, 0, tiled=True),
        lambda root: cut_root(root, core),
        (right_root[0],),
    )
    reduced = jnp.sum(arrived.astype(f32), axis=0).astype(bf16)

    spread = jnp.broadcast_to(reduced[None], (NZH * NZL,) + reduced.shape)
    column = lax.all_to_all(spread, ("zh", "zl"), 0, 0, tiled=True)
    column = column.reshape(NZH, NZL, band, half)

    want = owner_block[:, None, None, None]
    outgoing = jnp.where(
        want == 1, column[None, :, 1], jnp.where(want == 2, column[None, :, 2], column[None, :, 0])
    )
    mine, (where, source) = beside(
        outgoing.reshape(peers, NZH * band, half),
        lambda value: lax.all_to_all(value, DP, 0, 0, tiled=True),
        lambda owners: find(owners, shard, core, dp),
        (owner_block,),
    )
    mine = mine.reshape(peers, NZH, band, half).transpose(1, 0, 2, 3).reshape(NZH * rows, half)

    side = jnp.dot(left_root[0], mine, preferred_element_type=f32).astype(bf16)
    side_other = swap_cores(side)
    result = (
        jnp.dot(side, root_mine, preferred_element_type=f32)
        + jnp.dot(side_other, root_other, preferred_element_type=f32)
    ).astype(bf16)

    mine, result = lax.optimization_barrier((mine, result))
    other = swap_cores(mine)

    scattered = lax.all_to_all(result.reshape(peers, band, half), DP, 0, 0, tiled=True)
    placed = jnp.concatenate(
        [
            lax.dynamic_index_in_dim(scattered, source[block], 0, False)
            for block in range(blocks)
        ]
    )
    mine, other, placed = lax.optimization_barrier((mine, other, placed))
    new_left, new_right = update_stats(where, mine, other, left_stat[0], right_stat[0])
    spread = jnp.broadcast_to(placed[None], (peers,) + placed.shape)
    update_half = lax.all_to_all(spread, DP, 0, 0, tiled=True)
    update_half, new_left, new_right = lax.optimization_barrier((update_half, new_left, new_right))
    update_half = update_half.reshape(peers, blocks, band, half)
    update_half = update_half.transpose(1, 0, 2, 3).reshape(blocks, rows, half)
    update = join_halves(core[None].astype(jnp.int32), update_half, swap_cores(update_half))
    return update, new_left[None], new_right[None]


def solution(mesh):
    fine = Mesh(mesh.devices.reshape(NX, NY, NZH, NZL, NC), AXES)
    in_specs = (
        P(("x", "y", "zl", "c"), None, "zh", None),
        P(),
        P(DP, "zh", None),
        P(DP, "zh", None),
        P(DP, "zh", None),
        P(DP, None, None),
    )
    out_specs = (P(None, "zh", None), P(DP, "zh", None), P(DP, "zh", None))
    return jax.shard_map(
        per_device, mesh=fine, in_specs=in_specs, out_specs=out_specs, check_vma=False
    )
```

```python
import jax
import jax.numpy as jnp
from jax import lax
from jax.experimental import pallas as pl
from jax.experimental.pallas import tpu as pltpu
from jax.sharding import Mesh, PartitionSpec as P

BETA = 0.95
NX, NY = 4, 8
NZH, NZL, NC = 4, 3, 2
AXES = ("x", "y", "zh", "zl", "c")
DP = ("x", "y")


def swap_cores(value):
    return lax.ppermute(value, "c", [(0, 1), (1, 0)])


def beside(operand, transfer, work, inputs):
    operand, inputs = lax.optimization_barrier((operand, inputs))
    return lax.optimization_barrier((transfer(operand), work(*inputs)))


def stats_kernel(where, own, other, left_old, right_old, left_new, right_new, turned):
    shard, core, owns = where[0], where[1], where[2]
    rows = left_old.shape[0]
    half = own.shape[1]
    per_half = half // rows

    @pl.when(owns == 0)
    def _():
        left_new[...] = left_old[...]
        right_new[...] = right_old[...]

    @pl.when(owns != 0)
    def _():
        band = pl.ds(pl.multiple_of(shard * rows, rows), rows)
        outer = lax.dot_general(
            own[band, :], own[...], (((1,), (1,)), ((), ())), preferred_element_type=jnp.float32
        ) + lax.dot_general(
            other[band, :], other[...], (((1,), (1,)), ((), ())), preferred_element_type=jnp.float32
        )
        left_new[...] = BETA * left_old[...] + (1.0 - BETA) * outer
        columns = pl.ds(pl.multiple_of((shard % per_half) * rows, rows), rows)

        @pl.when(shard // per_half == core)
        def _():
            turned[...] = own[:, columns].T

        @pl.when(shard // per_half != core)
        def _():
            turned[...] = other[:, columns].T

        for source, place in ((own, core), (other, 1 - core)):
            span = pl.ds(pl.multiple_of(place * half, half), half)
            product = jnp.dot(turned[...], source[...], preferred_element_type=jnp.float32)
            right_new[:, span] = BETA * right_old[:, span] + (1.0 - BETA) * product


def update_stats(where, own, other, left_old, right_old):
    rows, width = left_old.shape
    vmem = pl.BlockSpec(memory_space=pltpu.VMEM)
    return pl.pallas_call(
        stats_kernel,
        out_shape=[jax.ShapeDtypeStruct((rows, width), jnp.float32)] * 2,
        in_specs=[pl.BlockSpec(memory_space=pltpu.SMEM)] + [vmem] * 4,
        out_specs=[vmem, vmem],
        scratch_shapes=[pltpu.VMEM((rows, width), jnp.bfloat16)],
        compiler_params=pltpu.CompilerParams(vmem_limit_bytes=24 * 1024 * 1024),
        cost_estimate=pl.CostEstimate(
            flops=4 * rows * width * width, bytes_accessed=24 * rows * width, transcendentals=0
        ),
    )(where, own, other, left_old, right_old)


def join_kernel(core, own, other, joined):
    half = own.shape[2]
    for source, place in ((own, core[0]), (other, 1 - core[0])):
        joined[:, :, pl.ds(pl.multiple_of(place * half, half), half)] = source[...]


def join_halves(core, own, other):
    blocks, rows, half = own.shape
    vmem = pl.BlockSpec(memory_space=pltpu.VMEM)
    return pl.pallas_call(
        join_kernel,
        out_shape=jax.ShapeDtypeStruct((blocks, rows, 2 * half), own.dtype),
        in_specs=[pl.BlockSpec(memory_space=pltpu.SMEM), vmem, vmem],
        out_specs=vmem,
        compiler_params=pltpu.CompilerParams(vmem_limit_bytes=16 * 1024 * 1024),
    )(core, own, other)


def cut_root(root, core):
    half = root.shape[1] // 2
    root = lax.dynamic_slice_in_dim(root, core * half, half, 1)
    return (
        lax.dynamic_slice_in_dim(root, core * half, half, 0),
        lax.dynamic_slice_in_dim(root, (1 - core) * half, half, 0),
    )


def find(owners, shard, core, dp):
    owns = (lax.dynamic_index_in_dim(owners, dp, 0, False) >= 0).astype(jnp.int32)
    where = jnp.stack([shard, core, owns]).astype(jnp.int32)
    hits = owners[None, :] == jnp.arange(NZL, dtype=jnp.int32)[:, None]
    return where, jnp.argmax(hits, axis=1).astype(jnp.int32)


def per_device(grads, owner_block, left_stat, right_stat, left_root, right_root):
    f32, bf16 = jnp.float32, jnp.bfloat16
    g = grads[0]
    blocks, rows, width = g.shape
    half = width // 2
    peers = NX * NY
    band = rows // peers
    core = lax.axis_index("c")
    shard = lax.axis_index("zh")
    dp = lax.axis_index(DP)
    first = core == 0

    low, high = g[:, :, :half], g[:, :, half:]
    got = swap_cores(jnp.where(first, high, low))
    pair = (jnp.where(first, low, high).astype(f32) + got.astype(f32)).astype(bf16)

    arrived = lax.all_to_all(
        pair.reshape(blocks * peers, band, half), ("zl",) + DP, 0, 0, tiled=True
    )
    reduced = jnp.sum(arrived.astype(f32), axis=0).astype(bf16)

    spread = jnp.broadcast_to(reduced[None], (NZH * NZL,) + reduced.shape)
    column, (root_mine, root_other, where, source) = beside(
        spread,
        lambda value: lax.all_to_all(value, ("zh", "zl"), 0, 0, tiled=True),
        lambda root, owners: cut_root(root, core) + find(owners, shard, core, dp),
        (right_root[0], owner_block),
    )
    column = column.reshape(NZH, NZL, band, half)

    want = owner_block[:, None, None, None]
    outgoing = jnp.where(
        want == 1, column[None, :, 1], jnp.where(want == 2, column[None, :, 2], column[None, :, 0])
    )
    mine = lax.all_to_all(outgoing.reshape(peers, NZH * band, half), DP, 0, 0, tiled=True)
    mine = mine.reshape(peers, NZH, band, half).transpose(1, 0, 2, 3).reshape(NZH * rows, half)

    side = jnp.dot(left_root[0], mine, preferred_element_type=f32).astype(bf16)
    side_other = swap_cores(side)
    result = (
        jnp.dot(side, root_mine, preferred_element_type=f32)
        + jnp.dot(side_other, root_other, preferred_element_type=f32)
    ).astype(bf16)


    scattered = lax.all_to_all(result.reshape(peers, band, half), DP, 0, 0, tiled=True)
    placed = jnp.concatenate(
        [
            lax.dynamic_index_in_dim(scattered, source[block], 0, False)
            for block in range(blocks)
        ]
    )
    mine, placed = lax.optimization_barrier((mine, placed))
    other = swap_cores(mine)
    new_left, new_right = update_stats(where, mine, other, left_stat[0], right_stat[0])
    spread = jnp.broadcast_to(placed[None], (peers,) + placed.shape)
    update_half = lax.all_to_all(spread, DP, 0, 0, tiled=True)
    update_half, new_left, new_right = lax.optimization_barrier((update_half, new_left, new_right))
    update_half = update_half.reshape(peers, blocks, band, half)
    update_half = update_half.transpose(1, 0, 2, 3).reshape(blocks, rows, half)
    update = join_halves(core[None].astype(jnp.int32), update_half, swap_cores(update_half))
    return update, new_left[None], new_right[None]


def solution(mesh):
    fine = Mesh(mesh.devices.reshape(NX, NY, NZH, NZL, NC), AXES)
    in_specs = (
        P(("x", "y", "zl", "c"), None, "zh", None),
        P(),
        P(DP, "zh", None),
        P(DP, "zh", None),
        P(DP, "zh", None),
        P(DP, None, None),
    )
    out_specs = (P(None, "zh", None), P(DP, "zh", None), P(DP, "zh", None))
    return jax.shard_map(
        per_device, mesh=fine, in_specs=in_specs, out_specs=out_specs, check_vma=False
    )
```

```python
import jax
import jax.numpy as jnp
from jax import lax
from jax.experimental import pallas as pl
from jax.experimental.pallas import tpu as pltpu
from jax.sharding import Mesh, PartitionSpec as P

BETA = 0.95
NX, NY = 4, 8
NZH, NZL, NC = 4, 3, 2
AXES = ("x", "y", "zh", "zl", "c")
DP = ("x", "y")


def swap_cores(value):
    return lax.ppermute(value, "c", [(0, 1), (1, 0)])


def beside(operand, transfer, work, inputs):
    operand, inputs = lax.optimization_barrier((operand, inputs))
    return lax.optimization_barrier((transfer(operand), work(*inputs)))


def stats_kernel(where, own, other, left_old, right_old, left_new, right_new, turned):
    shard, core, owns = where[0], where[1], where[2]
    rows = left_old.shape[0]
    half = own.shape[1]
    per_half = half // rows

    @pl.when(owns == 0)
    def _():
        left_new[...] = left_old[...]
        right_new[...] = right_old[...]

    @pl.when(owns != 0)
    def _():
        band = pl.ds(pl.multiple_of(shard * rows, rows), rows)
        outer = lax.dot_general(
            own[band, :], own[...], (((1,), (1,)), ((), ())), preferred_element_type=jnp.float32
        ) + lax.dot_general(
            other[band, :], other[...], (((1,), (1,)), ((), ())), preferred_element_type=jnp.float32
        )
        left_new[...] = BETA * left_old[...] + (1.0 - BETA) * outer
        columns = pl.ds(pl.multiple_of((shard % per_half) * rows, rows), rows)

        @pl.when(shard // per_half == core)
        def _():
            turned[...] = own[:, columns].T

        @pl.when(shard // per_half != core)
        def _():
            turned[...] = other[:, columns].T

        for source, place in ((own, core), (other, 1 - core)):
            span = pl.ds(pl.multiple_of(place * half, half), half)
            product = jnp.dot(turned[...], source[...], preferred_element_type=jnp.float32)
            right_new[:, span] = BETA * right_old[:, span] + (1.0 - BETA) * product


def update_stats(where, own, other, left_old, right_old):
    rows, width = left_old.shape
    vmem = pl.BlockSpec(memory_space=pltpu.VMEM)
    return pl.pallas_call(
        stats_kernel,
        out_shape=[jax.ShapeDtypeStruct((rows, width), jnp.float32)] * 2,
        in_specs=[pl.BlockSpec(memory_space=pltpu.SMEM)] + [vmem] * 4,
        out_specs=[vmem, vmem],
        scratch_shapes=[pltpu.VMEM((rows, width), jnp.bfloat16)],
        compiler_params=pltpu.CompilerParams(vmem_limit_bytes=24 * 1024 * 1024),
        cost_estimate=pl.CostEstimate(
            flops=4 * rows * width * width, bytes_accessed=24 * rows * width, transcendentals=0
        ),
    )(where, own, other, left_old, right_old)


def join_kernel(core, own, other, joined):
    peers, blocks, band, half = own.shape
    for source, place in ((own, core[0]), (other, 1 - core[0])):
        span = pl.ds(pl.multiple_of(place * half, half), half)
        for block in range(blocks):
            bands = source[:, block].astype(jnp.float32).reshape(peers * band, half)
            joined[block, :, span] = bands.astype(joined.dtype)


def join_halves(core, own, other):
    peers, blocks, band, half = own.shape
    vmem = pl.BlockSpec(memory_space=pltpu.VMEM)
    return pl.pallas_call(
        join_kernel,
        out_shape=jax.ShapeDtypeStruct((blocks, peers * band, 2 * half), own.dtype),
        in_specs=[pl.BlockSpec(memory_space=pltpu.SMEM), vmem, vmem],
        out_specs=vmem,
        compiler_params=pltpu.CompilerParams(vmem_limit_bytes=24 * 1024 * 1024),
    )(core, own, other)


def spread_kernel(source, scattered, spread):
    peers, blocks = spread.shape[:2]
    for block in range(blocks):
        piece = scattered[pl.ds(source[block], 1)]
        spread[:, block] = jnp.broadcast_to(piece, (peers,) + piece.shape[1:])


def spread_owned(source, scattered):
    peers, band, half = scattered.shape
    vmem = pl.BlockSpec(memory_space=pltpu.VMEM)
    return pl.pallas_call(
        spread_kernel,
        out_shape=jax.ShapeDtypeStruct((peers, NZL, band, half), scattered.dtype),
        in_specs=[pl.BlockSpec(memory_space=pltpu.SMEM), vmem],
        out_specs=vmem,
        compiler_params=pltpu.CompilerParams(vmem_limit_bytes=24 * 1024 * 1024),
    )(source, scattered)


def cut_root(root, core):
    half = root.shape[1] // 2
    root = lax.dynamic_slice_in_dim(root, core * half, half, 1)
    return (
        lax.dynamic_slice_in_dim(root, core * half, half, 0),
        lax.dynamic_slice_in_dim(root, (1 - core) * half, half, 0),
    )


def find(owners, shard, core, dp):
    owns = (lax.dynamic_index_in_dim(owners, dp, 0, False) >= 0).astype(jnp.int32)
    where = jnp.stack([shard, core, owns]).astype(jnp.int32)
    hits = owners[None, :] == jnp.arange(NZL, dtype=jnp.int32)[:, None]
    return where, jnp.argmax(hits, axis=1).astype(jnp.int32)


def per_device(grads, owner_block, left_stat, right_stat, left_root, right_root):
    f32, bf16 = jnp.float32, jnp.bfloat16
    g = grads[0]
    blocks, rows, width = g.shape
    half = width // 2
    peers = NX * NY
    band = rows // peers
    core = lax.axis_index("c")
    shard = lax.axis_index("zh")
    dp = lax.axis_index(DP)
    first = core == 0

    low, high = g[:, :, :half], g[:, :, half:]
    got = swap_cores(jnp.where(first, high, low))
    pair = (jnp.where(first, low, high).astype(f32) + got.astype(f32)).astype(bf16)

    arrived = lax.all_to_all(
        pair.reshape(blocks * peers, band, half), ("zl",) + DP, 0, 0, tiled=True
    )
    reduced = jnp.sum(arrived.astype(f32), axis=0).astype(bf16)

    spread = jnp.broadcast_to(reduced[None], (NZH * NZL,) + reduced.shape)
    column, (root_mine, root_other, where, source) = beside(
        spread,
        lambda value: lax.all_to_all(value, ("zh", "zl"), 0, 0, tiled=True),
        lambda root, owners: cut_root(root, core) + find(owners, shard, core, dp),
        (right_root[0], owner_block),
    )
    column = column.reshape(NZH, NZL, band, half)

    want = owner_block[:, None, None, None]
    outgoing = jnp.where(
        want == 1, column[None, :, 1], jnp.where(want == 2, column[None, :, 2], column[None, :, 0])
    )
    mine = lax.all_to_all(outgoing.reshape(peers, NZH * band, half), DP, 0, 0, tiled=True)
    mine = mine.reshape(peers, NZH, band, half).transpose(1, 0, 2, 3).reshape(NZH * rows, half)

    side = jnp.dot(left_root[0], mine, preferred_element_type=f32).astype(bf16)
    side_other = swap_cores(side)
    result = (
        jnp.dot(side, root_mine, preferred_element_type=f32)
        + jnp.dot(side_other, root_other, preferred_element_type=f32)
    ).astype(bf16)


    scattered = lax.all_to_all(result.reshape(peers, band, half), DP, 0, 0, tiled=True)
    spread = spread_owned(source, scattered)
    mine, spread = lax.optimization_barrier((mine, spread))
    other = swap_cores(mine)
    new_left, new_right = update_stats(where, mine, other, left_stat[0], right_stat[0])
    update_half = lax.all_to_all(spread, DP, 0, 0, tiled=True)
    update_half, new_left, new_right = lax.optimization_barrier((update_half, new_left, new_right))
    update = join_halves(core[None].astype(jnp.int32), update_half, swap_cores(update_half))
    return update, new_left[None], new_right[None]


def solution(mesh):
    fine = Mesh(mesh.devices.reshape(NX, NY, NZH, NZL, NC), AXES)
    in_specs = (
        P(("x", "y", "zl", "c"), None, "zh", None),
        P(),
        P(DP, "zh", None),
        P(DP, "zh", None),
        P(DP, "zh", None),
        P(DP, None, None),
    )
    out_specs = (P(None, "zh", None), P(DP, "zh", None), P(DP, "zh", None))
    return jax.shard_map(
        per_device, mesh=fine, in_specs=in_specs, out_specs=out_specs, check_vma=False
    )
```

```python
import jax
import jax.numpy as jnp
from jax import lax
from jax.experimental import pallas as pl
from jax.experimental.pallas import tpu as pltpu
from jax.sharding import Mesh, PartitionSpec as P

BETA = 0.95
NX, NY = 4, 8
NZH, NZL, NC = 4, 3, 2
AXES = ("x", "y", "zh", "zl", "c")
DP = ("x", "y")


def swap_cores(value):
    return lax.ppermute(value, "c", [(0, 1), (1, 0)])


def beside(operand, transfer, work, inputs):
    operand, inputs = lax.optimization_barrier((operand, inputs))
    return lax.optimization_barrier((transfer(operand), work(*inputs)))


def stats_kernel(where, own, other, left_old, right_old, left_new, right_new, turned):
    shard, core, owns = where[0], where[1], where[2]
    rows = left_old.shape[0]
    half = own.shape[1]
    per_half = half // rows

    @pl.when(owns == 0)
    def _():
        left_new[...] = left_old[...]
        right_new[...] = right_old[...]

    @pl.when(owns != 0)
    def _():
        band = pl.ds(pl.multiple_of(shard * rows, rows), rows)
        outer = lax.dot_general(
            own[band, :], own[...], (((1,), (1,)), ((), ())), preferred_element_type=jnp.float32
        ) + lax.dot_general(
            other[band, :], other[...], (((1,), (1,)), ((), ())), preferred_element_type=jnp.float32
        )
        left_new[...] = BETA * left_old[...] + (1.0 - BETA) * outer
        columns = pl.ds(pl.multiple_of((shard % per_half) * rows, rows), rows)

        @pl.when(shard // per_half == core)
        def _():
            turned[...] = own[:, columns].T

        @pl.when(shard // per_half != core)
        def _():
            turned[...] = other[:, columns].T

        for source, place in ((own, core), (other, 1 - core)):
            span = pl.ds(pl.multiple_of(place * half, half), half)
            product = jnp.dot(turned[...], source[...], preferred_element_type=jnp.float32)
            right_new[:, span] = BETA * right_old[:, span] + (1.0 - BETA) * product


def update_stats(where, own, other, left_old, right_old):
    rows, width = left_old.shape
    vmem = pl.BlockSpec(memory_space=pltpu.VMEM)
    return pl.pallas_call(
        stats_kernel,
        out_shape=[jax.ShapeDtypeStruct((rows, width), jnp.float32)] * 2,
        in_specs=[pl.BlockSpec(memory_space=pltpu.SMEM)] + [vmem] * 4,
        out_specs=[vmem, vmem],
        scratch_shapes=[pltpu.VMEM((rows, width), jnp.bfloat16)],
        compiler_params=pltpu.CompilerParams(vmem_limit_bytes=24 * 1024 * 1024),
        cost_estimate=pl.CostEstimate(
            flops=4 * rows * width * width, bytes_accessed=24 * rows * width, transcendentals=0
        ),
    )(where, own, other, left_old, right_old)


def join_kernel(core, own, other, joined):
    peers, blocks, band, half = own.shape
    for source, place in ((own, core[0]), (other, 1 - core[0])):
        span = pl.ds(pl.multiple_of(place * half, half), half)
        for block in range(blocks):
            bands = source[:, block].astype(jnp.float32).reshape(peers * band, half)
            joined[block, :, span] = bands.astype(joined.dtype)


def join_halves(core, own, other):
    peers, blocks, band, half = own.shape
    vmem = pl.BlockSpec(memory_space=pltpu.VMEM)
    return pl.pallas_call(
        join_kernel,
        out_shape=jax.ShapeDtypeStruct((blocks, peers * band, 2 * half), own.dtype),
        in_specs=[pl.BlockSpec(memory_space=pltpu.SMEM), vmem, vmem],
        out_specs=vmem,
        compiler_params=pltpu.CompilerParams(vmem_limit_bytes=24 * 1024 * 1024),
    )(core, own, other)


def spread_kernel(source, scattered, spread):
    peers, blocks = spread.shape[:2]
    for block in range(blocks):
        piece = scattered[pl.ds(source[block], 1)]
        spread[:, block] = jnp.broadcast_to(piece, (peers,) + piece.shape[1:])


def spread_owned(source, scattered):
    peers, band, half = scattered.shape
    vmem = pl.BlockSpec(memory_space=pltpu.VMEM)
    return pl.pallas_call(
        spread_kernel,
        out_shape=jax.ShapeDtypeStruct((peers, NZL, band, half), scattered.dtype),
        in_specs=[pl.BlockSpec(memory_space=pltpu.SMEM), vmem],
        out_specs=vmem,
        compiler_params=pltpu.CompilerParams(vmem_limit_bytes=24 * 1024 * 1024),
    )(source, scattered)


def cut_root(root, core):
    half = root.shape[1] // 2
    root = lax.dynamic_slice_in_dim(root, core * half, half, 1)
    return (
        lax.dynamic_slice_in_dim(root, core * half, half, 0),
        lax.dynamic_slice_in_dim(root, (1 - core) * half, half, 0),
    )


def find(owners, shard, core, dp):
    owns = (lax.dynamic_index_in_dim(owners, dp, 0, False) >= 0).astype(jnp.int32)
    where = jnp.stack([shard, core, owns]).astype(jnp.int32)
    hits = owners[None, :] == jnp.arange(NZL, dtype=jnp.int32)[:, None]
    return where, jnp.argmax(hits, axis=1).astype(jnp.int32)


def per_device(grads, owner_block, left_stat, right_stat, left_root, right_root):
    f32, bf16 = jnp.float32, jnp.bfloat16
    g = grads[0]
    blocks, rows, width = g.shape
    half = width // 2
    peers = NX * NY
    band = rows // peers
    core = lax.axis_index("c")
    shard = lax.axis_index("zh")
    dp = lax.axis_index(DP)
    first = core == 0

    low, high = g[:, :, :half], g[:, :, half:]
    got = swap_cores(jnp.where(first, high, low))
    pair = (jnp.where(first, low, high).astype(f32) + got.astype(f32)).astype(bf16)

    arrived, (root_mine, root_other, where, source) = beside(
        pair.reshape(blocks * peers, band, half),
        lambda value: lax.all_to_all(value, ("zl",) + DP, 0, 0, tiled=True),
        lambda root, owners: cut_root(root, core) + find(owners, shard, core, dp),
        (right_root[0], owner_block),
    )
    reduced = jnp.sum(arrived.astype(f32), axis=0).astype(bf16)

    spread = jnp.broadcast_to(reduced[None], (NZH * NZL,) + reduced.shape)
    column = lax.all_to_all(spread, ("zh", "zl"), 0, 0, tiled=True)
    column = column.reshape(NZH, NZL, band, half)

    want = owner_block[:, None, None, None]
    outgoing = jnp.where(
        want == 1, column[None, :, 1], jnp.where(want == 2, column[None, :, 2], column[None, :, 0])
    )
    mine = lax.all_to_all(outgoing.reshape(peers, NZH * band, half), DP, 0, 0, tiled=True)
    mine = mine.reshape(peers, NZH, band, half).transpose(1, 0, 2, 3).reshape(NZH * rows, half)

    side = jnp.dot(left_root[0], mine, preferred_element_type=f32).astype(bf16)
    side_other = swap_cores(side)
    result = (
        jnp.dot(side, root_mine, preferred_element_type=f32)
        + jnp.dot(side_other, root_other, preferred_element_type=f32)
    ).astype(bf16)


    scattered = lax.all_to_all(result.reshape(peers, band, half), DP, 0, 0, tiled=True)
    spread = spread_owned(source, scattered)
    mine, spread = lax.optimization_barrier((mine, spread))
    other = swap_cores(mine)
    new_left, new_right = update_stats(where, mine, other, left_stat[0], right_stat[0])
    update_half = lax.all_to_all(spread, DP, 0, 0, tiled=True)
    update_half, new_left, new_right = lax.optimization_barrier((update_half, new_left, new_right))
    update = join_halves(core[None].astype(jnp.int32), update_half, swap_cores(update_half))
    return update, new_left[None], new_right[None]


def solution(mesh):
    fine = Mesh(mesh.devices.reshape(NX, NY, NZH, NZL, NC), AXES)
    in_specs = (
        P(("x", "y", "zl", "c"), None, "zh", None),
        P(),
        P(DP, "zh", None),
        P(DP, "zh", None),
        P(DP, "zh", None),
        P(DP, None, None),
    )
    out_specs = (P(None, "zh", None), P(DP, "zh", None), P(DP, "zh", None))
    return jax.shard_map(
        per_device, mesh=fine, in_specs=in_specs, out_specs=out_specs, check_vma=False
    )
```

```python
import jax
import jax.numpy as jnp
from jax import lax
from jax.experimental import pallas as pl
from jax.experimental.pallas import tpu as pltpu
from jax.sharding import Mesh, PartitionSpec as P

BETA = 0.95
NX, NY = 4, 8
NZH, NZL, NC = 4, 3, 2
AXES = ("x", "y", "zh", "zl", "c")
DP = ("x", "y")
RING = ("y", "x")


def swap_cores(value):
    return lax.ppermute(value, "c", [(0, 1), (1, 0)])


def beside(operand, transfer, work, inputs):
    operand, inputs = lax.optimization_barrier((operand, inputs))
    return lax.optimization_barrier((transfer(operand), work(*inputs)))


def stats_kernel(where, own, other, left_old, right_old, left_new, right_new, turned):
    shard, core, owns = where[0], where[1], where[2]
    rows = left_old.shape[0]
    half = own.shape[1]
    per_half = half // rows

    @pl.when(owns == 0)
    def _():
        left_new[...] = left_old[...]
        right_new[...] = right_old[...]

    @pl.when(owns != 0)
    def _():
        band = pl.ds(pl.multiple_of(shard * rows, rows), rows)
        outer = lax.dot_general(
            own[band, :], own[...], (((1,), (1,)), ((), ())), preferred_element_type=jnp.float32
        ) + lax.dot_general(
            other[band, :], other[...], (((1,), (1,)), ((), ())), preferred_element_type=jnp.float32
        )
        left_new[...] = BETA * left_old[...] + (1.0 - BETA) * outer
        columns = pl.ds(pl.multiple_of((shard % per_half) * rows, rows), rows)

        @pl.when(shard // per_half == core)
        def _():
            turned[...] = own[:, columns].T

        @pl.when(shard // per_half != core)
        def _():
            turned[...] = other[:, columns].T

        for source, place in ((own, core), (other, 1 - core)):
            span = pl.ds(pl.multiple_of(place * half, half), half)
            product = jnp.dot(turned[...], source[...], preferred_element_type=jnp.float32)
            right_new[:, span] = BETA * right_old[:, span] + (1.0 - BETA) * product


def update_stats(where, own, other, left_old, right_old):
    rows, width = left_old.shape
    vmem = pl.BlockSpec(memory_space=pltpu.VMEM)
    return pl.pallas_call(
        stats_kernel,
        out_shape=[jax.ShapeDtypeStruct((rows, width), jnp.float32)] * 2,
        in_specs=[pl.BlockSpec(memory_space=pltpu.SMEM)] + [vmem] * 4,
        out_specs=[vmem, vmem],
        scratch_shapes=[pltpu.VMEM((rows, width), jnp.bfloat16)],
        compiler_params=pltpu.CompilerParams(vmem_limit_bytes=24 * 1024 * 1024),
        cost_estimate=pl.CostEstimate(
            flops=4 * rows * width * width, bytes_accessed=24 * rows * width, transcendentals=0
        ),
    )(where, own, other, left_old, right_old)


def join_kernel(core, own, other, joined):
    peers, blocks, band, half = own.shape
    for source, place in ((own, core[0]), (other, 1 - core[0])):
        span = pl.ds(pl.multiple_of(place * half, half), half)
        for block in range(blocks):
            bands = source[:, block].astype(jnp.float32).reshape(peers * band, half)
            joined[block, :, span] = bands.astype(joined.dtype)


def join_halves(core, own, other):
    peers, blocks, band, half = own.shape
    vmem = pl.BlockSpec(memory_space=pltpu.VMEM)
    return pl.pallas_call(
        join_kernel,
        out_shape=jax.ShapeDtypeStruct((blocks, peers * band, 2 * half), own.dtype),
        in_specs=[pl.BlockSpec(memory_space=pltpu.SMEM), vmem, vmem],
        out_specs=vmem,
        compiler_params=pltpu.CompilerParams(vmem_limit_bytes=24 * 1024 * 1024),
    )(core, own, other)


def spread_kernel(source, scattered, spread):
    peers, blocks = spread.shape[:2]
    for block in range(blocks):
        piece = scattered[pl.ds(source[block], 1)]
        spread[:, block] = jnp.broadcast_to(piece, (peers,) + piece.shape[1:])


def spread_owned(source, scattered):
    peers, band, half = scattered.shape
    vmem = pl.BlockSpec(memory_space=pltpu.VMEM)
    return pl.pallas_call(
        spread_kernel,
        out_shape=jax.ShapeDtypeStruct((peers, NZL, band, half), scattered.dtype),
        in_specs=[pl.BlockSpec(memory_space=pltpu.SMEM), vmem],
        out_specs=vmem,
        compiler_params=pltpu.CompilerParams(vmem_limit_bytes=24 * 1024 * 1024),
    )(source, scattered)


def cut_root(root, core):
    half = root.shape[1] // 2
    root = lax.dynamic_slice_in_dim(root, core * half, half, 1)
    return (
        lax.dynamic_slice_in_dim(root, core * half, half, 0),
        lax.dynamic_slice_in_dim(root, (1 - core) * half, half, 0),
    )


def find(owners, shard, core, dp):
    owns = (lax.dynamic_index_in_dim(owners, dp, 0, False) >= 0).astype(jnp.int32)
    where = jnp.stack([shard, core, owns]).astype(jnp.int32)
    hits = owners[None, :] == jnp.arange(NZL, dtype=jnp.int32)[:, None]
    return where, jnp.argmax(hits, axis=1).astype(jnp.int32)


def per_device(grads, owner_block, left_stat, right_stat, left_root, right_root):
    f32, bf16 = jnp.float32, jnp.bfloat16
    owner_block = owner_block.reshape(NX, NY).T.reshape(-1)
    g = grads[0]
    blocks, rows, width = g.shape
    half = width // 2
    peers = NX * NY
    band = rows // peers
    core = lax.axis_index("c")
    shard = lax.axis_index("zh")
    dp = lax.axis_index(RING)
    first = core == 0

    low, high = g[:, :, :half], g[:, :, half:]
    got = swap_cores(jnp.where(first, high, low))
    pair = (jnp.where(first, low, high).astype(f32) + got.astype(f32)).astype(bf16)

    arrived, (root_mine, root_other, where, source) = beside(
        pair.reshape(blocks * peers, band, half),
        lambda value: lax.all_to_all(value, ("zl",) + RING, 0, 0, tiled=True),
        lambda root, owners: cut_root(root, core) + find(owners, shard, core, dp),
        (right_root[0], owner_block),
    )
    reduced = jnp.sum(arrived.astype(f32), axis=0).astype(bf16)

    spread = jnp.broadcast_to(reduced[None], (NZH * NZL,) + reduced.shape)
    column = lax.all_to_all(spread, ("zh", "zl"), 0, 0, tiled=True)
    column = column.reshape(NZH, NZL, band, half)

    want = owner_block[:, None, None, None]
    outgoing = jnp.where(
        want == 1, column[None, :, 1], jnp.where(want == 2, column[None, :, 2], column[None, :, 0])
    )
    mine = lax.all_to_all(outgoing.reshape(peers, NZH * band, half), RING, 0, 0, tiled=True)
    mine = mine.reshape(peers, NZH, band, half).transpose(1, 0, 2, 3).reshape(NZH * rows, half)

    side = jnp.dot(left_root[0], mine, preferred_element_type=f32).astype(bf16)
    side_other = swap_cores(side)
    result = (
        jnp.dot(side, root_mine, preferred_element_type=f32)
        + jnp.dot(side_other, root_other, preferred_element_type=f32)
    ).astype(bf16)


    scattered = lax.all_to_all(result.reshape(peers, band, half), RING, 0, 0, tiled=True)
    spread = spread_owned(source, scattered)
    mine, spread = lax.optimization_barrier((mine, spread))
    other = swap_cores(mine)
    new_left, new_right = update_stats(where, mine, other, left_stat[0], right_stat[0])
    update_half = lax.all_to_all(spread, RING, 0, 0, tiled=True)
    update_half, new_left, new_right = lax.optimization_barrier((update_half, new_left, new_right))
    update = join_halves(core[None].astype(jnp.int32), update_half, swap_cores(update_half))
    return update, new_left[None], new_right[None]


def solution(mesh):
    fine = Mesh(mesh.devices.reshape(NX, NY, NZH, NZL, NC), AXES)
    in_specs = (
        P(("x", "y", "zl", "c"), None, "zh", None),
        P(),
        P(DP, "zh", None),
        P(DP, "zh", None),
        P(DP, "zh", None),
        P(DP, None, None),
    )
    out_specs = (P(None, "zh", None), P(DP, "zh", None), P(DP, "zh", None))
    return jax.shard_map(
        per_device, mesh=fine, in_specs=in_specs, out_specs=out_specs, check_vma=False
    )
```

```python
import jax
import jax.numpy as jnp
from jax import lax
from jax.experimental import pallas as pl
from jax.experimental.pallas import tpu as pltpu
from jax.sharding import Mesh, PartitionSpec as P

BETA = 0.95
NX, NY = 4, 8
NZH, NZL, NC = 4, 3, 2
AXES = ("x", "y", "zh", "zl", "c")
DP = ("x", "y")


def swap_cores(value):
    return lax.ppermute(value, "c", [(0, 1), (1, 0)])


def beside(operand, transfer, work, inputs):
    operand, inputs = lax.optimization_barrier((operand, inputs))
    return lax.optimization_barrier((transfer(operand), work(*inputs)))


def stats_kernel(where, own, other, left_old, right_old, left_new, right_new, turned):
    shard, core, owns = where[0], where[1], where[2]
    rows = left_old.shape[0]
    half = own.shape[1]
    per_half = half // rows

    @pl.when(owns == 0)
    def _():
        left_new[...] = left_old[...]
        right_new[...] = right_old[...]

    @pl.when(owns != 0)
    def _():
        band = pl.ds(pl.multiple_of(shard * rows, rows), rows)
        outer = lax.dot_general(
            own[band, :], own[...], (((1,), (1,)), ((), ())), preferred_element_type=jnp.float32
        ) + lax.dot_general(
            other[band, :], other[...], (((1,), (1,)), ((), ())), preferred_element_type=jnp.float32
        )
        left_new[...] = BETA * left_old[...] + (1.0 - BETA) * outer
        columns = pl.ds(pl.multiple_of((shard % per_half) * rows, rows), rows)

        @pl.when(shard // per_half == core)
        def _():
            turned[...] = own[:, columns].T

        @pl.when(shard // per_half != core)
        def _():
            turned[...] = other[:, columns].T

        for source, place in ((own, core), (other, 1 - core)):
            span = pl.ds(pl.multiple_of(place * half, half), half)
            product = jnp.dot(turned[...], source[...], preferred_element_type=jnp.float32)
            right_new[:, span] = BETA * right_old[:, span] + (1.0 - BETA) * product


def update_stats(where, own, other, left_old, right_old):
    rows, width = left_old.shape
    vmem = pl.BlockSpec(memory_space=pltpu.VMEM)
    return pl.pallas_call(
        stats_kernel,
        out_shape=[jax.ShapeDtypeStruct((rows, width), jnp.float32)] * 2,
        in_specs=[pl.BlockSpec(memory_space=pltpu.SMEM)] + [vmem] * 4,
        out_specs=[vmem, vmem],
        scratch_shapes=[pltpu.VMEM((rows, width), jnp.bfloat16)],
        compiler_params=pltpu.CompilerParams(vmem_limit_bytes=24 * 1024 * 1024),
        cost_estimate=pl.CostEstimate(
            flops=4 * rows * width * width, bytes_accessed=24 * rows * width, transcendentals=0
        ),
    )(where, own, other, left_old, right_old)


def join_kernel(core, own, other, joined):
    peers, blocks, band, half = own.shape
    for source, place in ((own, core[0]), (other, 1 - core[0])):
        span = pl.ds(pl.multiple_of(place * half, half), half)
        for block in range(blocks):
            bands = source[:, block].astype(jnp.float32).reshape(peers * band, half)
            joined[block, :, span] = bands.astype(joined.dtype)


def join_halves(core, own, other):
    peers, blocks, band, half = own.shape
    vmem = pl.BlockSpec(memory_space=pltpu.VMEM)
    return pl.pallas_call(
        join_kernel,
        out_shape=jax.ShapeDtypeStruct((blocks, peers * band, 2 * half), own.dtype),
        in_specs=[pl.BlockSpec(memory_space=pltpu.SMEM), vmem, vmem],
        out_specs=vmem,
        compiler_params=pltpu.CompilerParams(vmem_limit_bytes=24 * 1024 * 1024),
    )(core, own, other)


def spread_kernel(source, scattered, spread):
    peers, blocks = spread.shape[:2]
    for block in range(blocks):
        piece = scattered[pl.ds(source[block], 1)]
        spread[:, block] = jnp.broadcast_to(piece, (peers,) + piece.shape[1:])


def spread_owned(source, scattered):
    peers, band, half = scattered.shape
    vmem = pl.BlockSpec(memory_space=pltpu.VMEM)
    return pl.pallas_call(
        spread_kernel,
        out_shape=jax.ShapeDtypeStruct((peers, NZL, band, half), scattered.dtype),
        in_specs=[pl.BlockSpec(memory_space=pltpu.SMEM), vmem],
        out_specs=vmem,
        compiler_params=pltpu.CompilerParams(vmem_limit_bytes=24 * 1024 * 1024),
    )(source, scattered)


def cut_root(root, core):
    half = root.shape[1] // 2
    root = lax.dynamic_slice_in_dim(root, core * half, half, 1)
    return (
        lax.dynamic_slice_in_dim(root, core * half, half, 0),
        lax.dynamic_slice_in_dim(root, (1 - core) * half, half, 0),
    )


def find(owners, shard, core, dp):
    owns = (lax.dynamic_index_in_dim(owners, dp, 0, False) >= 0).astype(jnp.int32)
    where = jnp.stack([shard, core, owns]).astype(jnp.int32)
    hits = owners[None, :] == jnp.arange(NZL, dtype=jnp.int32)[:, None]
    return where, jnp.argmax(hits, axis=1).astype(jnp.int32)


def per_device(grads, owner_block, left_stat, right_stat, left_root, right_root):
    f32, bf16 = jnp.float32, jnp.bfloat16
    g = grads[0]
    blocks, rows, width = g.shape
    half = width // 2
    peers = NX * NY
    band = rows // peers
    core = lax.axis_index("c")
    shard = lax.axis_index("zh")
    dp = lax.axis_index(DP)
    first = core == 0

    low, high = g[:, :, :half], g[:, :, half:]
    got = swap_cores(jnp.where(first, high, low))
    pair = (jnp.where(first, low, high).astype(f32) + got.astype(f32)).astype(bf16)

    arrived, (root_mine, root_other, where, source) = beside(
        pair.reshape(blocks * peers, band, half),
        lambda value: lax.all_to_all(value, ("zl",) + DP, 0, 0, tiled=True),
        lambda root, owners: cut_root(root, core) + find(owners, shard, core, dp),
        (right_root[0], owner_block),
    )
    reduced = jnp.sum(arrived.astype(f32), axis=0).astype(bf16)

    spread = jnp.broadcast_to(reduced[None], (NZH * NZL,) + reduced.shape)
    column = lax.all_to_all(spread, ("zh", "zl"), 0, 0, tiled=True)
    column = column.reshape(NZH, NZL, band, half)

    want = owner_block[:, None, None, None]
    outgoing = jnp.where(
        want == 1, column[None, :, 1], jnp.where(want == 2, column[None, :, 2], column[None, :, 0])
    )
    mine = lax.all_to_all(outgoing.reshape(peers, NZH * band, half), DP, 0, 0, tiled=True)
    mine = mine.reshape(peers, NZH, band, half).transpose(1, 0, 2, 3).reshape(NZH * rows, half)

    side = jnp.dot(left_root[0], mine, preferred_element_type=f32).astype(bf16)
    side_other = swap_cores(side)
    result = (
        jnp.dot(side, root_mine, preferred_element_type=f32)
        + jnp.dot(side_other, root_other, preferred_element_type=f32)
    ).astype(bf16)


    scattered, (new_left, new_right) = beside(
        result.reshape(peers, band, half),
        lambda value: lax.all_to_all(value, DP, 0, 0, tiled=True),
        lambda own: update_stats(where, own, swap_cores(own), left_stat[0], right_stat[0]),
        (mine,),
    )
    spread = spread_owned(source, scattered)
    update_half = lax.all_to_all(spread, DP, 0, 0, tiled=True)
    update = join_halves(core[None].astype(jnp.int32), update_half, swap_cores(update_half))
    return update, new_left[None], new_right[None]


def solution(mesh):
    fine = Mesh(mesh.devices.reshape(NX, NY, NZH, NZL, NC), AXES)
    in_specs = (
        P(("x", "y", "zl", "c"), None, "zh", None),
        P(),
        P(DP, "zh", None),
        P(DP, "zh", None),
        P(DP, "zh", None),
        P(DP, None, None),
    )
    out_specs = (P(None, "zh", None), P(DP, "zh", None), P(DP, "zh", None))
    return jax.shard_map(
        per_device, mesh=fine, in_specs=in_specs, out_specs=out_specs, check_vma=False
    )
```

```python
import jax
import jax.numpy as jnp
from jax import lax
from jax.experimental import pallas as pl
from jax.experimental.pallas import tpu as pltpu
from jax.sharding import Mesh, PartitionSpec as P

BETA = 0.95
NX, NY = 4, 8
NZH, NZL, NC = 4, 3, 2
AXES = ("x", "y", "zh", "zl", "c")
DP = ("x", "y")


def swap_cores(value):
    return lax.ppermute(value, "c", [(0, 1), (1, 0)])


def beside(operand, transfer, work, inputs):
    operand, inputs = lax.optimization_barrier((operand, inputs))
    return lax.optimization_barrier((transfer(operand), work(*inputs)))


def stats_kernel(where, own, other, left_old, right_old, left_new, right_new, turned):
    shard, core, owns = where[0], where[1], where[2]
    rows = left_old.shape[0]
    half = own.shape[1]
    per_half = half // rows

    @pl.when(owns == 0)
    def _():
        left_new[...] = left_old[...]
        right_new[...] = right_old[...]

    @pl.when(owns != 0)
    def _():
        band = pl.ds(pl.multiple_of(shard * rows, rows), rows)
        outer = lax.dot_general(
            own[band, :], own[...], (((1,), (1,)), ((), ())), preferred_element_type=jnp.float32
        ) + lax.dot_general(
            other[band, :], other[...], (((1,), (1,)), ((), ())), preferred_element_type=jnp.float32
        )
        left_new[...] = BETA * left_old[...] + (1.0 - BETA) * outer
        columns = pl.ds(pl.multiple_of((shard % per_half) * rows, rows), rows)

        @pl.when(shard // per_half == core)
        def _():
            turned[...] = own[:, columns].T

        @pl.when(shard // per_half != core)
        def _():
            turned[...] = other[:, columns].T

        for source, place in ((own, core), (other, 1 - core)):
            span = pl.ds(pl.multiple_of(place * half, half), half)
            product = jnp.dot(turned[...], source[...], preferred_element_type=jnp.float32)
            right_new[:, span] = BETA * right_old[:, span] + (1.0 - BETA) * product


def update_stats(where, own, other, left_old, right_old):
    rows, width = left_old.shape
    vmem = pl.BlockSpec(memory_space=pltpu.VMEM)
    return pl.pallas_call(
        stats_kernel,
        out_shape=[jax.ShapeDtypeStruct((rows, width), jnp.float32)] * 2,
        in_specs=[pl.BlockSpec(memory_space=pltpu.SMEM)] + [vmem] * 4,
        out_specs=[vmem, vmem],
        scratch_shapes=[pltpu.VMEM((rows, width), jnp.bfloat16)],
        compiler_params=pltpu.CompilerParams(vmem_limit_bytes=24 * 1024 * 1024),
        cost_estimate=pl.CostEstimate(
            flops=4 * rows * width * width, bytes_accessed=24 * rows * width, transcendentals=0
        ),
    )(where, own, other, left_old, right_old)


def join_kernel(core, own, other, joined):
    peers, blocks, band, half = own.shape
    for source, place in ((own, core[0]), (other, 1 - core[0])):
        span = pl.ds(pl.multiple_of(place * half, half), half)
        for block in range(blocks):
            bands = source[:, block].astype(jnp.float32).reshape(peers * band, half)
            joined[block, :, span] = bands.astype(joined.dtype)


def join_halves(core, own, other):
    peers, blocks, band, half = own.shape
    vmem = pl.BlockSpec(memory_space=pltpu.VMEM)
    return pl.pallas_call(
        join_kernel,
        out_shape=jax.ShapeDtypeStruct((blocks, peers * band, 2 * half), own.dtype),
        in_specs=[pl.BlockSpec(memory_space=pltpu.SMEM), vmem, vmem],
        out_specs=vmem,
        compiler_params=pltpu.CompilerParams(vmem_limit_bytes=24 * 1024 * 1024),
    )(core, own, other)


def spread_kernel(source, scattered, spread):
    peers, blocks = spread.shape[:2]
    for block in range(blocks):
        piece = scattered[pl.ds(source[block], 1)]
        spread[:, block] = jnp.broadcast_to(piece, (peers,) + piece.shape[1:])


def spread_owned(source, scattered):
    peers, band, half = scattered.shape
    vmem = pl.BlockSpec(memory_space=pltpu.VMEM)
    return pl.pallas_call(
        spread_kernel,
        out_shape=jax.ShapeDtypeStruct((peers, NZL, band, half), scattered.dtype),
        in_specs=[pl.BlockSpec(memory_space=pltpu.SMEM), vmem],
        out_specs=vmem,
        compiler_params=pltpu.CompilerParams(vmem_limit_bytes=24 * 1024 * 1024),
    )(source, scattered)


def cut_root(root, core):
    half = root.shape[1] // 2
    root = lax.dynamic_slice_in_dim(root, core * half, half, 1)
    return (
        lax.dynamic_slice_in_dim(root, core * half, half, 0),
        lax.dynamic_slice_in_dim(root, (1 - core) * half, half, 0),
    )


def find(owners, shard, core, dp):
    owns = (lax.dynamic_index_in_dim(owners, dp, 0, False) >= 0).astype(jnp.int32)
    where = jnp.stack([shard, core, owns]).astype(jnp.int32)
    hits = owners[None, :] == jnp.arange(NZL, dtype=jnp.int32)[:, None]
    return where, jnp.argmax(hits, axis=1).astype(jnp.int32)


def per_device(grads, owner_block, left_stat, right_stat, left_root, right_root):
    f32, bf16 = jnp.float32, jnp.bfloat16
    g = grads[0]
    blocks, rows, width = g.shape
    half = width // 2
    peers = NX * NY
    band = rows // peers
    core = lax.axis_index("c")
    shard = lax.axis_index("zh")
    dp = lax.axis_index(DP)
    first = core == 0

    low, high = g[:, :, :half], g[:, :, half:]
    got = swap_cores(jnp.where(first, high, low))
    pair = (jnp.where(first, low, high).astype(f32) + got.astype(f32)).astype(bf16)

    pieces = pair.reshape(blocks, NX, rows // NX, half).transpose(1, 0, 2, 3)
    arrived = lax.all_to_all(pieces.reshape(NX, -1, half), "x", 0, 0, tiled=True)
    quarter = jnp.sum(arrived.astype(f32), axis=0).astype(bf16)

    arrived, (root_mine, root_other, where, source) = beside(
        quarter.reshape(blocks * NY, band, half),
        lambda value: lax.all_to_all(value, ("zl", "y"), 0, 0, tiled=True),
        lambda root, owners: cut_root(root, core) + find(owners, shard, core, dp),
        (right_root[0], owner_block),
    )
    reduced = jnp.sum(arrived.astype(f32), axis=0).astype(bf16)

    spread = jnp.broadcast_to(reduced[None], (NZH * NZL,) + reduced.shape)
    column = lax.all_to_all(spread, ("zh", "zl"), 0, 0, tiled=True)
    column = column.reshape(NZH, NZL, band, half)

    want = owner_block[:, None, None, None]
    outgoing = jnp.where(
        want == 1, column[None, :, 1], jnp.where(want == 2, column[None, :, 2], column[None, :, 0])
    )
    mine = lax.all_to_all(outgoing.reshape(peers, NZH * band, half), DP, 0, 0, tiled=True)
    mine = mine.reshape(peers, NZH, band, half).transpose(1, 0, 2, 3).reshape(NZH * rows, half)

    side = jnp.dot(left_root[0], mine, preferred_element_type=f32).astype(bf16)
    side_other = swap_cores(side)
    result = (
        jnp.dot(side, root_mine, preferred_element_type=f32)
        + jnp.dot(side_other, root_other, preferred_element_type=f32)
    ).astype(bf16)


    scattered = lax.all_to_all(result.reshape(peers, band, half), DP, 0, 0, tiled=True)
    spread = spread_owned(source, scattered)
    mine, spread = lax.optimization_barrier((mine, spread))
    other = swap_cores(mine)
    new_left, new_right = update_stats(where, mine, other, left_stat[0], right_stat[0])
    update_half = lax.all_to_all(spread, DP, 0, 0, tiled=True)
    update_half, new_left, new_right = lax.optimization_barrier((update_half, new_left, new_right))
    update = join_halves(core[None].astype(jnp.int32), update_half, swap_cores(update_half))
    return update, new_left[None], new_right[None]


def solution(mesh):
    fine = Mesh(mesh.devices.reshape(NX, NY, NZH, NZL, NC), AXES)
    in_specs = (
        P(("x", "y", "zl", "c"), None, "zh", None),
        P(),
        P(DP, "zh", None),
        P(DP, "zh", None),
        P(DP, "zh", None),
        P(DP, None, None),
    )
    out_specs = (P(None, "zh", None), P(DP, "zh", None), P(DP, "zh", None))
    return jax.shard_map(
        per_device, mesh=fine, in_specs=in_specs, out_specs=out_specs, check_vma=False
    )
```

```python
import jax
import jax.numpy as jnp
from jax import lax
from jax.experimental import pallas as pl
from jax.experimental.pallas import tpu as pltpu
from jax.sharding import Mesh, PartitionSpec as P

BETA = 0.95
NX, NY = 4, 8
NZH, NZL, NC = 4, 3, 2
AXES = ("x", "y", "zh", "zl", "c")
DP = ("x", "y")


def swap_cores(value):
    return lax.ppermute(value, "c", [(0, 1), (1, 0)])


def beside(operand, transfer, work, inputs):
    operand, inputs = lax.optimization_barrier((operand, inputs))
    return lax.optimization_barrier((transfer(operand), work(*inputs)))


def stats_kernel(where, own, other, left_old, right_old, left_new, right_new, turned):
    shard, core, owns = where[0], where[1], where[2]
    rows = left_old.shape[0]
    half = own.shape[1]
    per_half = half // rows

    @pl.when(owns == 0)
    def _():
        left_new[...] = left_old[...]
        right_new[...] = right_old[...]

    @pl.when(owns != 0)
    def _():
        band = pl.ds(pl.multiple_of(shard * rows, rows), rows)
        outer = lax.dot_general(
            own[band, :], own[...], (((1,), (1,)), ((), ())), preferred_element_type=jnp.float32
        ) + lax.dot_general(
            other[band, :], other[...], (((1,), (1,)), ((), ())), preferred_element_type=jnp.float32
        )
        left_new[...] = BETA * left_old[...] + (1.0 - BETA) * outer
        columns = pl.ds(pl.multiple_of((shard % per_half) * rows, rows), rows)

        @pl.when(shard // per_half == core)
        def _():
            turned[...] = own[:, columns].T

        @pl.when(shard // per_half != core)
        def _():
            turned[...] = other[:, columns].T

        for source, place in ((own, core), (other, 1 - core)):
            span = pl.ds(pl.multiple_of(place * half, half), half)
            product = jnp.dot(turned[...], source[...], preferred_element_type=jnp.float32)
            right_new[:, span] = BETA * right_old[:, span] + (1.0 - BETA) * product


def update_stats(where, own, other, left_old, right_old):
    rows, width = left_old.shape
    vmem = pl.BlockSpec(memory_space=pltpu.VMEM)
    return pl.pallas_call(
        stats_kernel,
        out_shape=[jax.ShapeDtypeStruct((rows, width), jnp.float32)] * 2,
        in_specs=[pl.BlockSpec(memory_space=pltpu.SMEM)] + [vmem] * 4,
        out_specs=[vmem, vmem],
        scratch_shapes=[pltpu.VMEM((rows, width), jnp.bfloat16)],
        compiler_params=pltpu.CompilerParams(vmem_limit_bytes=24 * 1024 * 1024),
        cost_estimate=pl.CostEstimate(
            flops=4 * rows * width * width, bytes_accessed=24 * rows * width, transcendentals=0
        ),
    )(where, own, other, left_old, right_old)


def join_kernel(core, own, other, joined):
    peers, blocks, band, half = own.shape
    for source, place in ((own, core[0]), (other, 1 - core[0])):
        span = pl.ds(pl.multiple_of(place * half, half), half)
        for block in range(blocks):
            bands = source[:, block].astype(jnp.float32).reshape(peers * band, half)
            joined[block, :, span] = bands.astype(joined.dtype)


def join_halves(core, own, other):
    peers, blocks, band, half = own.shape
    vmem = pl.BlockSpec(memory_space=pltpu.VMEM)
    return pl.pallas_call(
        join_kernel,
        out_shape=jax.ShapeDtypeStruct((blocks, peers * band, 2 * half), own.dtype),
        in_specs=[pl.BlockSpec(memory_space=pltpu.SMEM), vmem, vmem],
        out_specs=vmem,
        compiler_params=pltpu.CompilerParams(vmem_limit_bytes=24 * 1024 * 1024),
    )(core, own, other)


def spread_kernel(source, scattered, spread):
    peers, blocks = spread.shape[:2]
    for block in range(blocks):
        piece = scattered[pl.ds(source[block], 1)]
        spread[:, block] = jnp.broadcast_to(piece, (peers,) + piece.shape[1:])


def spread_owned(source, scattered):
    _, band, half = scattered.shape
    vmem = pl.BlockSpec(memory_space=pltpu.VMEM)
    return pl.pallas_call(
        spread_kernel,
        out_shape=jax.ShapeDtypeStruct((NY, NZL, band, half), scattered.dtype),
        in_specs=[pl.BlockSpec(memory_space=pltpu.SMEM), vmem],
        out_specs=vmem,
        compiler_params=pltpu.CompilerParams(vmem_limit_bytes=24 * 1024 * 1024),
    )(source, scattered)


def cut_root(root, core):
    half = root.shape[1] // 2
    root = lax.dynamic_slice_in_dim(root, core * half, half, 1)
    return (
        lax.dynamic_slice_in_dim(root, core * half, half, 0),
        lax.dynamic_slice_in_dim(root, (1 - core) * half, half, 0),
    )


def find(owners, shard, core, dp):
    owns = (lax.dynamic_index_in_dim(owners, dp, 0, False) >= 0).astype(jnp.int32)
    where = jnp.stack([shard, core, owns]).astype(jnp.int32)
    hits = owners[None, :] == jnp.arange(NZL, dtype=jnp.int32)[:, None]
    return where, jnp.argmax(hits, axis=1).astype(jnp.int32)


def per_device(grads, owner_block, left_stat, right_stat, left_root, right_root):
    f32, bf16 = jnp.float32, jnp.bfloat16
    g = grads[0]
    blocks, rows, width = g.shape
    half = width // 2
    peers = NX * NY
    band = rows // peers
    core = lax.axis_index("c")
    shard = lax.axis_index("zh")
    dp = lax.axis_index(DP)
    first = core == 0

    low, high = g[:, :, :half], g[:, :, half:]
    got = swap_cores(jnp.where(first, high, low))
    pair = (jnp.where(first, low, high).astype(f32) + got.astype(f32)).astype(bf16)

    pieces = pair.reshape(blocks, NX, rows // NX, half).transpose(1, 0, 2, 3)
    arrived = lax.all_to_all(pieces.reshape(NX, -1, half), "x", 0, 0, tiled=True)
    quarter = jnp.sum(arrived.astype(f32), axis=0).astype(bf16)

    arrived, (root_mine, root_other, where, source) = beside(
        quarter.reshape(blocks * NY, band, half),
        lambda value: lax.all_to_all(value, ("zl", "y"), 0, 0, tiled=True),
        lambda root, owners: cut_root(root, core) + find(owners, shard, core, dp),
        (right_root[0], owner_block),
    )
    reduced = jnp.sum(arrived.astype(f32), axis=0).astype(bf16)

    spread = jnp.broadcast_to(reduced[None], (NZH * NZL,) + reduced.shape)
    column = lax.all_to_all(spread, ("zh", "zl"), 0, 0, tiled=True)
    column = column.reshape(NZH, NZL, band, half)

    want = owner_block[:, None, None, None]
    outgoing = jnp.where(
        want == 1, column[None, :, 1], jnp.where(want == 2, column[None, :, 2], column[None, :, 0])
    )
    mine = lax.all_to_all(outgoing.reshape(peers, NZH * band, half), DP, 0, 0, tiled=True)
    mine = mine.reshape(peers, NZH, band, half).transpose(1, 0, 2, 3).reshape(NZH * rows, half)

    side = jnp.dot(left_root[0], mine, preferred_element_type=f32).astype(bf16)
    side_other = swap_cores(side)
    result = (
        jnp.dot(side, root_mine, preferred_element_type=f32)
        + jnp.dot(side_other, root_other, preferred_element_type=f32)
    ).astype(bf16)


    scattered = lax.all_to_all(result.reshape(peers, band, half), DP, 0, 0, tiled=True)
    spread = spread_owned(source, scattered)
    along_y, other = beside(
        spread, lambda value: lax.all_to_all(value, "y", 0, 0, tiled=True), swap_cores, (mine,)
    )
    spread = jnp.broadcast_to(along_y[None], (NX,) + along_y.shape)
    update_half, (new_left, new_right) = beside(
        spread.reshape(NX, -1, half),
        lambda value: lax.all_to_all(value, "x", 0, 0, tiled=True),
        lambda *halves: update_stats(where, *halves, left_stat[0], right_stat[0]),
        (mine, other),
    )
    update_half = update_half.reshape(peers, blocks, band, half)
    update = join_halves(core[None].astype(jnp.int32), update_half, swap_cores(update_half))
    return update, new_left[None], new_right[None]


def solution(mesh):
    fine = Mesh(mesh.devices.reshape(NX, NY, NZH, NZL, NC), AXES)
    in_specs = (
        P(("x", "y", "zl", "c"), None, "zh", None),
        P(),
        P(DP, "zh", None),
        P(DP, "zh", None),
        P(DP, "zh", None),
        P(DP, None, None),
    )
    out_specs = (P(None, "zh", None), P(DP, "zh", None), P(DP, "zh", None))
    return jax.shard_map(
        per_device, mesh=fine, in_specs=in_specs, out_specs=out_specs, check_vma=False
    )
```
